512 devices in a mesh: band: 16 (over z_lo, y), tok: 32 (over x, z_hi, core).
Axes of the slice: x: 4, y: 8, z: 8 (z_hi: 4, z_lo: 2; z = z_hi * 2 + z_lo), core: 2. Of those that a mesh axis runs over, the one named last changes fastest.
Arguments:
- latents: bfloat16 [256, 1024, 1152], P('band', 'tok'), may hold values from -6 to 6
- new_frame: bfloat16 [1024, 1152], P('tok'), may hold values from -6 to 6
- levels: int32 [256], P('band'), may hold values from 0 to 255, as said below
- timesteps: int32 [256], replicated, may hold values from 0 to 999, as said below
- mod_table: float32 [2, 1152], replicated, may hold values from -3 to 3
- w_query: bfloat16 [1152, 576], replicated
- w_key: bfloat16 [1152, 576], replicated
- w_value: bfloat16 [1152, 576], replicated, may hold values from -0.1875 to 0.1875
Outputs:
- queued: bfloat16 [256, 1024, 1152], P('band', 'tok')
- attended: bfloat16 [256, 1024, 576], P('band', 'tok')
The draws below stay inside these ranges and needn't reach their ends.
Inputs may be any that keep to these rules, and one draw needn't show every extreme that they name: `levels`: non-decreasing along the queue. `timesteps`: non-increasing in the level.
All inputs are finite; a program needn't handle non-finite values.
Results may differ from the reference program's by a relative error of at most 0.0056.
Values may be sent and summed in bfloat16 or wider, within the bound.
No kernel may reach another device: no remote copies, remote signals or barrier semaphores. Data moves between devices by JAX's collectives and lax.ppermute only.
A program may use at most 192 MiB of HBM per device.

```python
import math
import jax
import jax.numpy as jnp
from jax import lax

D = 1152
HEADS = 8
HD = 72
FRAMES = 256
LEVELS = 256
TOK_FRAME = 1024


def draw_levels(key, part):
    key = jax.random.fold_in(key, 11)
    steps = jax.random.randint(key, (FRAMES,), 1, 3)
    running = jnp.cumsum(steps) - steps
    return jnp.minimum(running, LEVELS - 1).astype(jnp.int32)


def draw_timesteps(key, part):
    key = jax.random.fold_in(key, 12)
    picked = jax.random.randint(key, (LEVELS,), 0, 1000)
    ordered = -jnp.sort(-picked)
    ordered = ordered.at[0].set(999)
    ordered = ordered.at[LEVELS - 1].set(0)
    return ordered.astype(jnp.int32)


def draw_w_query(key, part):
    key = jax.random.fold_in(key, 21)
    return (jax.random.normal(key, (D, HEADS * HD), jnp.float32) / math.sqrt(D)).astype(jnp.bfloat16)


def draw_w_key(key, part):
    key = jax.random.fold_in(key, 22)
    return (jax.random.normal(key, (D, HEADS * HD), jnp.float32) / math.sqrt(D)).astype(jnp.bfloat16)


def steps_of(rng, dims, cuts, smallest, high):
    gain, own = 1.0, jax.random.fold_in(rng, 6)
    for dim, parts in cuts:
        heights = jnp.exp(jax.random.uniform(jax.random.fold_in(own, dim), (parts,), jnp.float32, smallest / len(cuts), high / len(cuts)))
        gain = gain * jnp.repeat(heights, dims[dim] // parts).reshape([-1 if axis == dim else 1 for axis in range(len(dims))])
    return gain


def noise(key, shape, scale, most, shards=(), kind=jnp.bfloat16):
    drawn = scale * jax.random.normal(key, shape, jnp.float32)
    if shards:
        drawn = drawn * steps_of(key, shape, shards, -0.22, 0.18)
    return jnp.clip(drawn, -most, most).astype(kind)


def setup_inputs(seed: int = 0) -> dict:
    key_of = jax.random.split(jax.random.key(seed), 9)
    return {
        "latents": noise(key_of[0], (FRAMES, TOK_FRAME, D), 1.0, 6.0, ((0, 16), (1, 32))),
        "new_frame": noise(key_of[1], (TOK_FRAME, D), 1.0, 6.0, ((0, 32),)),
        "levels": draw_levels(jax.random.fold_in(key_of[8], 71), 0),
        "timesteps": draw_timesteps(jax.random.fold_in(key_of[8], 71), 0),
        "mod_table": noise(key_of[4], (2, D), 0.5, 3.0, (), jnp.float32),
        "w_query": draw_w_query(jax.random.fold_in(key_of[8], 71), 0),
        "w_key": draw_w_key(jax.random.fold_in(key_of[8], 71), 0),
        "w_value": noise(key_of[7], (D, HEADS * HD), D ** -0.5, 0.1875),
    }


def modulation(levels, timesteps, mod_table):
    level_count = timesteps.shape[0]
    one_hot = (levels[:, None] == jnp.arange(level_count, dtype=jnp.int32)[None, :]).astype(jnp.int32)
    noise_time = lax.optimization_barrier(jnp.sum(one_hot * timesteps[None, :], axis=1)).astype(jnp.float32)
    feature_count = mod_table.shape[1]
    frequency = jnp.exp(-math.log(10000.0) * jnp.arange(feature_count, dtype=jnp.float32) / feature_count)
    phases = noise_time[:, None] * frequency[None, :]
    offset = mod_table[0][None, :] + jnp.cos(phases)
    stretch = mod_table[1][None, :] + jnp.sin(phases)
    return (offset, stretch)

def normalize(queued, offset, stretch):
    values_f = queued.astype(jnp.float32)
    average = lax.optimization_barrier(jnp.mean(values_f, axis=-1, keepdims=True))
    centred = values_f - average
    spread = lax.optimization_barrier(jnp.mean(centred * centred, axis=-1, keepdims=True))
    normed = centred * lax.rsqrt(spread + 1e-06)
    return (normed * (1.0 + stretch[:, None, :]) + offset[:, None, :]).astype(jnp.bfloat16)

def attend_frame(operands):
    query_f, key_f, value_f = operands
    token_count = query_f.shape[0]
    query_h = query_f.reshape(token_count, HEADS, HD).astype(jnp.float32)
    key_h = key_f.reshape(token_count, HEADS, HD).astype(jnp.float32)
    value_h = value_f.reshape(token_count, HEADS, HD).astype(jnp.float32)
    scores = jnp.einsum('shd,khd->hsk', query_h, key_h) / math.sqrt(HD)
    peak = lax.optimization_barrier(jnp.max(scores, axis=-1, keepdims=True))
    expo = jnp.exp(scores - peak)
    attn_weights = (expo / lax.optimization_barrier(jnp.sum(expo, axis=-1, keepdims=True))).astype(jnp.bfloat16)
    result = jnp.einsum('hsk,khd->shd', attn_weights.astype(jnp.float32), value_h)
    return result.reshape(token_count, HEADS * HD).astype(jnp.bfloat16)

def reference(latents, new_frame, levels, timesteps, mod_table, w_query, w_key, w_value):
    queued = jnp.concatenate([new_frame[None], latents[:-1]], axis=0)
    offset, stretch = modulation(levels, timesteps, mod_table)
    normed = normalize(queued, offset, stretch).reshape(FRAMES * TOK_FRAME, D)
    query_proj = jnp.dot(normed, w_query, preferred_element_type=jnp.float32).astype(jnp.bfloat16)
    key_proj = jnp.dot(normed, w_key, preferred_element_type=jnp.float32).astype(jnp.bfloat16)
    value_proj = jnp.dot(normed, w_value, preferred_element_type=jnp.float32).astype(jnp.bfloat16)
    shaped = (FRAMES, TOK_FRAME, HEADS * HD)
    attended = lax.map(attend_frame, (query_proj.reshape(shaped), key_proj.reshape(shaped), value_proj.reshape(shaped)))
    return (queued, attended)
```

```python
import functools
import math

import jax
import jax.numpy as jnp
from jax import lax
from jax.experimental import pallas as pl
from jax.experimental.pallas import tpu as pltpu
from jax.sharding import PartitionSpec as P

HEADS = 8
HD = 72
LANE = 128
SCALE_LOG2 = math.log2(math.e) / math.sqrt(HD)


def from_behind(block, axis, distance):
    devices = range(lax.axis_size(axis))
    route = [(i - distance, i) for i in devices if i - distance in devices]
    return lax.ppermute(block, axis, route)


def modulation(levels, timesteps, mod_table):
    level_count = timesteps.shape[0]
    one_hot = (levels[:, None] == jnp.arange(level_count, dtype=jnp.int32)[None, :]).astype(
        jnp.int32
    )
    noise_time = jnp.sum(one_hot * timesteps[None, :], axis=1).astype(jnp.float32)
    feature_count = mod_table.shape[1]
    frequency = jnp.exp(
        -math.log(10000.0) * jnp.arange(feature_count, dtype=jnp.float32) / feature_count
    )
    phases = noise_time[:, None] * frequency[None, :]
    offset = mod_table[0][None, :] + jnp.cos(phases)
    stretch = mod_table[1][None, :] + jnp.sin(phases)
    return (offset, stretch)


def normalize(queued, offset, stretch):
    values_f = queued.astype(jnp.float32)
    average = jnp.mean(values_f, axis=-1, keepdims=True)
    centred = values_f - average
    spread = jnp.mean(centred * centred, axis=-1, keepdims=True)
    normed = centred * lax.rsqrt(spread + 1e-06)
    return (normed * (1.0 + stretch[:, None, :]) + offset[:, None, :]).astype(jnp.bfloat16)


def pad_heads(weight):
    per_head = weight.reshape(weight.shape[0], HEADS, HD)
    return jnp.pad(per_head, ((0, 0), (0, 0), (0, LANE - HD))).reshape(weight.shape[0], -1)


def project(normed, weight):
    return jnp.dot(normed, weight, preferred_element_type=jnp.float32)


def attention_kernel(query_ref, own_ref, other_ref, out_ref):
    dims = (((1,), (1,)), ((), ()))
    width = HEADS * LANE
    for head in range(HEADS):
        cols = pl.ds(head * LANE, LANE)
        value_cols = pl.ds(width + head * LANE, LANE)
        query = query_ref[:, cols]
        score_a = lax.dot_general(
            query, own_ref[:, cols], dims, preferred_element_type=jnp.float32
        )
        score_b = lax.dot_general(
            query, other_ref[:, cols], dims, preferred_element_type=jnp.float32
        )
        peak = jnp.maximum(
            jnp.max(score_a, axis=1, keepdims=True), jnp.max(score_b, axis=1, keepdims=True)
        )
        weight_a = jnp.exp2((score_a - peak) * SCALE_LOG2).astype(jnp.bfloat16)
        weight_b = jnp.exp2((score_b - peak) * SCALE_LOG2).astype(jnp.bfloat16)
        total = jnp.dot(weight_a, own_ref[:, value_cols], preferred_element_type=jnp.float32)
        total += jnp.dot(weight_b, other_ref[:, value_cols], preferred_element_type=jnp.float32)
        out_ref[:, pl.ds(head * HD, HD)] = (total[:, :HD] / total[:, HD : HD + 1]).astype(
            out_ref.dtype
        )


def attend(query, own, other):
    rows = query.shape[0]
    vmem = pl.BlockSpec(memory_space=pltpu.VMEM)
    return pl.pallas_call(
        attention_kernel,
        out_shape=jax.ShapeDtypeStruct((rows, HEADS * HD), jnp.bfloat16),
        in_specs=[vmem] * 3,
        out_specs=vmem,
        compiler_params=pltpu.CompilerParams(vmem_limit_bytes=48 * 2**20),
        name="attention",
    )(query, own, other)


def shards(latents, new_frame, levels, timesteps, mod_table, w_query, w_key, w_value):
    frames, tokens_dev, model_width = latents.shape
    groups = lax.axis_size("tok")
    incoming = from_behind(latents[-1:], "band", 1)
    head_frame = jnp.where(lax.axis_index("band") == 0, new_frame[None], incoming)
    queued = jnp.concatenate([head_frame, latents[:-1]], axis=0)
    offset, stretch = modulation(levels, timesteps, mod_table)
    normed = normalize(queued, offset, stretch)
    sent = normed.reshape(groups, frames * tokens_dev // groups, model_width)
    mine = lax.all_to_all(sent, "tok", split_axis=0, concat_axis=0, tiled=True)
    mine = mine.reshape(frames * tokens_dev, model_width)
    w_pair = jnp.concatenate([pad_heads(w_key), pad_heads(w_value)], axis=1)
    lane = jnp.arange(2 * HEADS * LANE)
    ones = ((lane >= HEADS * LANE) & (lane % LANE == HD)).astype(jnp.float32)
    own = (project(mine, w_pair) + ones[None, :]).astype(jnp.bfloat16)
    other = lax.ppermute(own, "tok", [(i, i ^ 1) for i in range(groups)])
    query = project(mine, pad_heads(w_query)).astype(jnp.bfloat16)
    result = attend(query, own, other)
    back = lax.all_to_all(
        result.reshape(groups, -1, HEADS * HD), "tok", split_axis=0, concat_axis=0, tiled=True
    )
    return (queued, back.reshape(frames, tokens_dev, HEADS * HD))


def solution(mesh):
    in_specs = (P("band", "tok", None), P("tok", None), P("band"), P(), P(), P(), P(), P())
    out_specs = (P("band", "tok", None), P("band", "tok", None))
    return jax.shard_map(shards, mesh=mesh, in_specs=in_specs, out_specs=out_specs, check_vma=False)
```

```python
import functools
import math

import jax
import jax.numpy as jnp
from jax import lax
from jax.experimental import pallas as pl
from jax.experimental.pallas import tpu as pltpu
from jax.sharding import PartitionSpec as P

HEADS = 8
HD = 72
LANE = 128
WIDTH = 640
SCALE_LOG2 = math.log2(math.e) / math.sqrt(HD)


def from_behind(block, axis, distance):
    devices = range(lax.axis_size(axis))
    route = [(i - distance, i) for i in devices if i - distance in devices]
    return lax.ppermute(block, axis, route)


def modulation(levels, timesteps, mod_table):
    level_count = timesteps.shape[0]
    one_hot = (levels[:, None] == jnp.arange(level_count, dtype=jnp.int32)[None, :]).astype(
        jnp.int32
    )
    noise_time = jnp.sum(one_hot * timesteps[None, :], axis=1).astype(jnp.float32)
    feature_count = mod_table.shape[1]
    frequency = jnp.exp(
        -math.log(10000.0) * jnp.arange(feature_count, dtype=jnp.float32) / feature_count
    )
    phases = noise_time[:, None] * frequency[None, :]
    offset = mod_table[0][None, :] + jnp.cos(phases)
    stretch = mod_table[1][None, :] + jnp.sin(phases)
    return (offset, stretch)


def project_kernel(tokens_ref, stretch_ref, offset_ref, weight_ref, query_ref, pair_ref):
    rows = tokens_ref.shape[0]
    step = 128
    parts = []
    for start in range(0, rows, step):
        values = tokens_ref[pl.ds(start, step), :].astype(jnp.float32)
        average = jnp.mean(values, axis=-1, keepdims=True)
        centred = values - average
        spread = jnp.mean(centred * centred, axis=-1, keepdims=True)
        normed = centred * lax.rsqrt(spread + 1e-06)
        parts.append(
            (normed * (1.0 + stretch_ref[...]) + offset_ref[...]).astype(jnp.bfloat16)
        )
    normed = jnp.concatenate(parts, axis=0)
    pair_cols = pair_ref.shape[1]
    pair_ref[...] = jnp.dot(
        normed, weight_ref[:, :pair_cols], preferred_element_type=jnp.float32
    ).astype(jnp.bfloat16)
    query_ref[...] = jnp.dot(
        normed, weight_ref[:, pair_cols:], preferred_element_type=jnp.float32
    ).astype(jnp.bfloat16)


def normalize_and_project(tokens, stretch, offset, weight):
    vmem = pl.BlockSpec(memory_space=pltpu.VMEM)
    rows = tokens.shape[0]
    return pl.pallas_call(
        project_kernel,
        out_shape=(
            jax.ShapeDtypeStruct((rows, WIDTH), jnp.bfloat16),
            jax.ShapeDtypeStruct((rows, 2 * WIDTH), jnp.bfloat16),
        ),
        in_specs=[vmem] * 4,
        out_specs=(vmem, vmem),
        compiler_params=pltpu.CompilerParams(vmem_limit_bytes=24 * 2**20),
        name="project",
    )(tokens, stretch, offset, weight)


def attention_kernel(query_ref, pair_ref, out_ref):
    dims = (((1,), (1,)), ((), ()))
    window = 2 * LANE
    rows, keys = query_ref.shape[0], pair_ref.shape[0]
    lane_q = lax.broadcasted_iota(jnp.int32, (rows, window), 1)
    lane_k = lax.broadcasted_iota(jnp.int32, (keys, window), 1)
    done = None
    for head in range(HEADS):
        start = head * HD // LANE * LANE
        first = head * HD - start
        query = query_ref[:, pl.ds(start, window)]
        key = pair_ref[:, pl.ds(start, window)]
        value = pair_ref[:, pl.ds(WIDTH + start, window)]
        query = jnp.where((lane_q >= first) & (lane_q < first + HD), query, 0)
        value = jnp.where((lane_k >= first) & (lane_k < first + HD), value, 1)
        score = lax.dot_general(query, key, dims, preferred_element_type=jnp.float32)
        peak = jnp.max(score, axis=1, keepdims=True)
        weight = jnp.exp2((score - peak) * SCALE_LOG2).astype(jnp.bfloat16)
        total = jnp.dot(weight, value, preferred_element_type=jnp.float32)
        at = first + HD if first + HD < window else 0
        result = total / total[:, at : at + 1]
        if done is None:
            done = result
        else:
            if start != done_start:
                out_ref[:, pl.ds(done_start, LANE)] = done[:, :LANE].astype(out_ref.dtype)
                done = jnp.concatenate([done[:, LANE:], result[:, LANE:]], axis=1)
            done = jnp.where(lane_q < first, done, result)
        done_start = start
    tail = HEADS * HD - done_start
    out_ref[:, pl.ds(done_start, tail)] = done[:, :tail].astype(out_ref.dtype)


def attend(query, pair):
    vmem = pl.BlockSpec(memory_space=pltpu.VMEM)
    return pl.pallas_call(
        attention_kernel,
        out_shape=jax.ShapeDtypeStruct((query.shape[0], HEADS * HD), jnp.bfloat16),
        in_specs=[vmem] * 2,
        out_specs=vmem,
        compiler_params=pltpu.CompilerParams(vmem_limit_bytes=32 * 2**20),
        name="attention",
    )(query, pair)


def shards(latents, new_frame, levels, timesteps, mod_table, w_query, w_key, w_value):
    frames, tokens_dev, model_width = latents.shape
    groups = lax.axis_size("tok")
    cores = groups // frames
    same_core = [[cores * i + core for i in range(frames)] for core in range(cores)]
    same_chip = [[cores * i + core for core in range(cores)] for i in range(frames)]
    incoming = from_behind(latents[-1:], "band", 1)
    head_frame = jnp.where(lax.axis_index("band") == 0, new_frame[None], incoming)
    queued = jnp.concatenate([head_frame, latents[:-1]], axis=0)
    mine = lax.all_to_all(
        queued, "tok", split_axis=0, concat_axis=0, axis_index_groups=same_core, tiled=True
    )
    mine = mine.reshape(frames * tokens_dev, model_width)
    level = lax.dynamic_slice_in_dim(levels, lax.axis_index("tok") // cores, 1)
    offset, stretch = modulation(level, timesteps, mod_table)
    gap = jnp.zeros((model_width, WIDTH - HEADS * HD), w_key.dtype)
    weights = jnp.concatenate([w_key, gap, w_value, gap, w_query, gap], axis=1)
    query, own = normalize_and_project(mine, stretch, offset, weights)
    pair = lax.all_gather(own, "tok", axis=0, axis_index_groups=same_chip, tiled=True)
    result = attend(query, pair)
    back = lax.all_to_all(
        result.reshape(frames, tokens_dev, HEADS * HD),
        "tok",
        split_axis=0,
        concat_axis=0,
        axis_index_groups=same_core,
        tiled=True,
    )
    return (queued, back)


def solution(mesh):
    in_specs = (P("band", "tok", None), P("tok", None), P("band"), P(), P(), P(), P(), P())
    out_specs = (P("band", "tok", None), P("band", "tok", None))
    return jax.shard_map(shards, mesh=mesh, in_specs=in_specs, out_specs=out_specs, check_vma=False)
```

```python
import functools
import math

import jax
import jax.numpy as jnp
from jax import lax
from jax.experimental import pallas as pl
from jax.experimental.pallas import tpu as pltpu
from jax.sharding import PartitionSpec as P

HEADS = 8
HD = 72
LANE = 128
WIDTH = 640
SCALE_LOG2 = math.log2(math.e) / math.sqrt(HD)


def from_behind(block, axis, distance):
    devices = range(lax.axis_size(axis))
    route = [(i - distance, i) for i in devices if i - distance in devices]
    return lax.ppermute(block, axis, route)


def modulation(levels, timesteps, mod_table):
    level_count = timesteps.shape[0]
    one_hot = (levels[:, None] == jnp.arange(level_count, dtype=jnp.int32)[None, :]).astype(
        jnp.int32
    )
    noise_time = jnp.sum(one_hot * timesteps[None, :], axis=1).astype(jnp.float32)
    feature_count = mod_table.shape[1]
    frequency = jnp.exp(
        -math.log(10000.0) * jnp.arange(feature_count, dtype=jnp.float32) / feature_count
    )
    phases = noise_time[:, None] * frequency[None, :]
    offset = mod_table[0][None, :] + jnp.cos(phases)
    stretch = mod_table[1][None, :] + jnp.sin(phases)
    return (offset, stretch)


def project_kernel(
    tokens_ref, stretch_ref, offset_ref, weight_hbm, normed_ref, pair_ref, weight_ref, arrived
):
    rows, depth = tokens_ref.shape
    pieces = arrived.shape[0]
    piece = depth // pieces
    copies = [
        pltpu.make_async_copy(
            weight_hbm.at[pl.ds(i * piece, piece)],
            weight_ref.at[pl.ds(i * piece, piece)],
            arrived.at[i],
        )
        for i in range(pieces)
    ]
    for copy in copies:
        copy.start()
    half, step = rows // 2, 64

    def normalized(first):
        parts = []
        for start in range(first, first + half, step):
            values = tokens_ref[pl.ds(start, step), :].astype(jnp.float32)
            average = jnp.mean(values, axis=-1, keepdims=True)
            centred = values - average
            spread = jnp.mean(centred * centred, axis=-1, keepdims=True)
            normed = centred * lax.rsqrt(spread + 1e-06)
            parts.append(
                (normed * (1.0 + stretch_ref[...]) + offset_ref[...]).astype(jnp.bfloat16)
            )
        normed = jnp.concatenate(parts, axis=0)
        normed_ref[pl.ds(first, half), :] = normed
        return normed

    def project(normed, first):
        pair_ref[pl.ds(first, half), :] = jnp.dot(
            normed, weight_ref[...], preferred_element_type=jnp.float32
        ).astype(jnp.bfloat16)

    upper = normalized(0)
    for copy in copies:
        copy.wait()
    project(upper, 0)
    project(normalized(half), half)


def normalize_and_project(tokens, stretch, offset, weight):
    vmem = pl.BlockSpec(memory_space=pltpu.VMEM)
    rows, width = tokens.shape[0], weight.shape[1]
    return pl.pallas_call(
        project_kernel,
        out_shape=(
            jax.ShapeDtypeStruct(tokens.shape, jnp.bfloat16),
            jax.ShapeDtypeStruct((rows, width), jnp.bfloat16),
        ),
        in_specs=[vmem] * 3 + [pl.BlockSpec(memory_space=pltpu.HBM)],
        out_specs=(vmem, vmem),
        scratch_shapes=[
            pltpu.VMEM(weight.shape, jnp.bfloat16),
            pltpu.SemaphoreType.DMA((4,)),
        ],
        compiler_params=pltpu.CompilerParams(vmem_limit_bytes=24 * 2**20),
        name="project",
    )(tokens, stretch, offset, weight)


def attention_kernel(query_ref, own_ref, other_ref, out_ref):
    dims = (((1,), (1,)), ((), ()))
    window = 2 * LANE
    rows = query_ref.shape[0]
    lane = lax.broadcasted_iota(jnp.int32, (rows, window), 1)
    for head in range(HEADS):
        start = head * HD // LANE * LANE
        first = head * HD - start
        inside = (lane >= first) & (lane < first + HD)
        query = jnp.where(inside, query_ref[:, pl.ds(start, window)], 0)
        scores = [
            lax.dot_general(
                query, pair[:, pl.ds(start, window)], dims, preferred_element_type=jnp.float32
            )
            for pair in (own_ref, other_ref)
        ]
        peak = jnp.maximum(*(jnp.max(score, axis=1, keepdims=True) for score in scores))
        total = 0.0
        for score, pair in zip(scores, (own_ref, other_ref)):
            weight = jnp.exp2((score - peak) * SCALE_LOG2).astype(jnp.bfloat16)
            value = jnp.where(inside, pair[:, pl.ds(WIDTH + start, window)], 1)
            total += jnp.dot(weight, value, preferred_element_type=jnp.float32)
        at = first + HD if first + HD < window else 0
        result = total / total[:, at : at + 1]
        if head == 0:
            done = result
        else:
            if start != done_start:
                out_ref[:, pl.ds(done_start, LANE)] = done[:, :LANE].astype(out_ref.dtype)
                done = jnp.concatenate([done[:, LANE:], result[:, LANE:]], axis=1)
            done = jnp.where(lane < first, done, result)
        done_start = start
    tail = HEADS * HD - done_start
    out_ref[:, pl.ds(done_start, tail)] = done[:, :tail].astype(out_ref.dtype)


def attend(query, own, other):
    vmem = pl.BlockSpec(memory_space=pltpu.VMEM)
    return pl.pallas_call(
        attention_kernel,
        out_shape=jax.ShapeDtypeStruct((query.shape[0], HEADS * HD), jnp.bfloat16),
        in_specs=[vmem] * 3,
        out_specs=vmem,
        compiler_params=pltpu.CompilerParams(vmem_limit_bytes=32 * 2**20),
        name="attention",
    )(query, own, other)


def shards(latents, new_frame, levels, timesteps, mod_table, w_query, w_key, w_value):
    frames, tokens_dev, model_width = latents.shape
    groups = lax.axis_size("tok")
    cores = groups // frames
    same_core = [[cores * i + core for i in range(frames)] for core in range(cores)]
    incoming = from_behind(latents[-1:], "band", 1)
    head_frame = jnp.where(lax.axis_index("band") == 0, new_frame[None], incoming)
    moved = lax.optimization_barrier(jnp.concatenate([new_frame[None], latents[:-1]], axis=0))
    queued = lax.dynamic_update_slice_in_dim(moved, head_frame, 0, axis=0)
    mine = lax.all_to_all(
        queued, "tok", split_axis=0, concat_axis=0, axis_index_groups=same_core, tiled=True
    )
    mine = mine.reshape(frames * tokens_dev, model_width)
    level = lax.dynamic_slice_in_dim(levels, lax.axis_index("tok") // cores, 1)
    offset, stretch = modulation(level, timesteps, mod_table)
    gap = jnp.zeros((model_width, WIDTH - HEADS * HD), w_key.dtype)
    w_pair = jnp.concatenate([w_key, gap, w_value, gap], axis=1)
    normed, own = normalize_and_project(mine, stretch, offset, w_pair)
    other = lax.ppermute(own, "tok", [(i, i ^ 1) for i in range(groups)])
    query = jnp.dot(
        normed, jnp.concatenate([w_query, gap], axis=1), preferred_element_type=jnp.float32
    ).astype(jnp.bfloat16)
    result = attend(query, own, other)
    back = lax.all_to_all(
        result.reshape(frames, tokens_dev, HEADS * HD),
        "tok",
        split_axis=0,
        concat_axis=0,
        axis_index_groups=same_core,
        tiled=True,
    )
    return (queued, back)


def solution(mesh):
    in_specs = (P("band", "tok", None), P("tok", None), P("band"), P(), P(), P(), P(), P())
    out_specs = (P("band", "tok", None), P("band", "tok", None))
    return jax.shard_map(shards, mesh=mesh, in_specs=in_specs, out_specs=out_specs, check_vma=False)
```

```python
import functools
import math

import jax
import jax.numpy as jnp
from jax import lax
from jax.experimental import pallas as pl
from jax.experimental.pallas import tpu as pltpu
from jax.sharding import PartitionSpec as P

HEADS = 8
HD = 72
LANE = 128
WIDTH = HEADS * HD
SHIFT = WIDTH % LANE
SCALE_LOG2 = math.log2(math.e) / math.sqrt(HD)


def from_behind(block, axis, distance):
    devices = range(lax.axis_size(axis))
    route = [(i - distance, i) for i in devices if i - distance in devices]
    return lax.ppermute(block, axis, route)


def modulation(levels, timesteps, mod_table):
    level_count = timesteps.shape[0]
    one_hot = (levels[:, None] == jnp.arange(level_count, dtype=jnp.int32)[None, :]).astype(
        jnp.int32
    )
    noise_time = jnp.sum(one_hot * timesteps[None, :], axis=1).astype(jnp.float32)
    feature_count = mod_table.shape[1]
    frequency = jnp.exp(
        -math.log(10000.0) * jnp.arange(feature_count, dtype=jnp.float32) / feature_count
    )
    phases = noise_time[:, None] * frequency[None, :]
    offset = mod_table[0][None, :] + jnp.cos(phases)
    stretch = mod_table[1][None, :] + jnp.sin(phases)
    return (offset, stretch)


def project_kernel(
    tokens_hbm, stretch_ref, offset_ref, weight_ref, normed_ref, pair_ref, tokens_ref, arrived
):
    rows = tokens_ref.shape[0]
    step = 128
    copies = [
        pltpu.make_async_copy(
            tokens_hbm.at[pl.ds(i * step, step)], tokens_ref.at[pl.ds(i * step, step)], arrived.at[i]
        )
        for i in range(rows // step)
    ]
    for copy in copies:
        copy.start()
    parts = []
    for i in range(rows // step):
        copies[i].wait()
        values = tokens_ref[pl.ds(i * step, step), :].astype(jnp.float32)
        average = jnp.mean(values, axis=-1, keepdims=True)
        centred = values - average
        spread = jnp.mean(centred * centred, axis=-1, keepdims=True)
        normed = centred * lax.rsqrt(spread + 1e-06)
        normed = (normed * (1.0 + stretch_ref[...]) + offset_ref[...]).astype(jnp.bfloat16)
        normed_ref[pl.ds(i * step, step), :] = normed
        parts.append(normed)
    pair_ref[...] = jnp.dot(
        jnp.concatenate(parts, axis=0), weight_ref[...], preferred_element_type=jnp.float32
    ).astype(jnp.bfloat16)


def normalize_and_project(tokens, stretch, offset, weight):
    vmem = pl.BlockSpec(memory_space=pltpu.VMEM)
    rows, width = tokens.shape[0], weight.shape[1]
    return pl.pallas_call(
        project_kernel,
        out_shape=(
            jax.ShapeDtypeStruct(tokens.shape, jnp.bfloat16),
            jax.ShapeDtypeStruct((rows, width), jnp.bfloat16),
        ),
        in_specs=[pl.BlockSpec(memory_space=pl.ANY)] + [vmem] * 3,
        out_specs=(vmem, vmem),
        scratch_shapes=[
            pltpu.VMEM(tokens.shape, jnp.bfloat16),
            pltpu.SemaphoreType.DMA((rows // 128,)),
        ],
        compiler_params=pltpu.CompilerParams(vmem_limit_bytes=24 * 2**20),
        name="project",
    )(tokens, stretch, offset, weight)


def attention_kernel(query_ref, own_ref, other_ref, out_ref):
    dims = (((1,), (1,)), ((), ()))
    window = 2 * LANE
    rows = query_ref.shape[0]
    lane = lax.broadcasted_iota(jnp.int32, (rows, window), 1)
    pairs = (own_ref, other_ref)
    for head in range(HEADS):
        start = min((SHIFT + head * HD) // LANE * LANE, SHIFT + WIDTH - window)
        first = SHIFT + head * HD - start
        inside = (lane >= first) & (lane < first + HD)
        query = jnp.where(inside, query_ref[:, pl.ds(start, window)], 0)
        scores = [
            lax.dot_general(
                query,
                pair[:, pl.ds(WIDTH - SHIFT + start, window)],
                dims,
                preferred_element_type=jnp.float32,
            )
            for pair in pairs
        ]
        peak = jnp.maximum(*(jnp.max(score, axis=1, keepdims=True) for score in scores))
        start = head * HD // LANE * LANE
        first = head * HD - start
        inside = (lane >= first) & (lane < first + HD)
        total = 0.0
        for score, pair in zip(scores, pairs):
            weight = jnp.exp2((score - peak) * SCALE_LOG2).astype(jnp.bfloat16)
            value = jnp.where(inside, pair[:, pl.ds(start, window)], 1)
            total += jnp.dot(weight, value, preferred_element_type=jnp.float32)
        at = first + HD if first + HD < window else 0
        result = total / total[:, at : at + 1]
        if head == 0:
            done = result
        else:
            if start != done_start:
                out_ref[:, pl.ds(done_start, LANE)] = done[:, :LANE].astype(jnp.bfloat16)
                done = jnp.concatenate([done[:, LANE:], result[:, LANE:]], axis=1)
            done = jnp.where(lane < first, done, result)
        done_start = start
    tail = WIDTH - done_start
    out_ref[:, pl.ds(done_start, tail)] = done[:, :tail].astype(jnp.bfloat16)


def attend(query, own, other):
    vmem = pl.BlockSpec(memory_space=pltpu.VMEM)
    rows = query.shape[0]
    return pl.pallas_call(
        attention_kernel,
        out_shape=jax.ShapeDtypeStruct((rows, WIDTH), jnp.bfloat16),
        in_specs=[vmem] * 3,
        out_specs=vmem,
        compiler_params=pltpu.CompilerParams(vmem_limit_bytes=32 * 2**20),
        name="attention",
    )(query, own, other)


def shards(latents, new_frame, levels, timesteps, mod_table, w_query, w_key, w_value):
    frames, tokens_dev, model_width = latents.shape
    groups = lax.axis_size("tok")
    cores = groups // frames
    same_core = [[cores * i + core for i in range(frames)] for core in range(cores)]
    incoming = from_behind(latents[-1:], "band", 1)
    head_frame = jnp.where(lax.axis_index("band") == 0, new_frame[None], incoming)
    moved = lax.optimization_barrier(jnp.concatenate([new_frame[None], latents[:-1]], axis=0))
    queued = lax.dynamic_update_slice_in_dim(moved, head_frame, 0, axis=0)
    mine = lax.all_to_all(
        queued, "tok", split_axis=0, concat_axis=0, axis_index_groups=same_core, tiled=True
    )
    mine = mine.reshape(frames * tokens_dev, model_width)
    level = lax.dynamic_slice_in_dim(levels, lax.axis_index("tok") // cores, 1)
    offset, stretch = modulation(level, timesteps, mod_table)
    w_pair = jnp.concatenate([w_value, w_key], axis=1)
    normed, own = normalize_and_project(mine, stretch, offset, w_pair)
    other = lax.ppermute(own, "tok", [(i, i ^ 1) for i in range(groups)])
    w_shifted = jnp.pad(w_query, ((0, 0), (SHIFT, 0)))
    query = jnp.dot(normed, w_shifted, preferred_element_type=jnp.float32).astype(jnp.bfloat16)
    result = attend(query, own, other)
    attended = lax.all_to_all(
        result.reshape(frames, tokens_dev, WIDTH),
        "tok",
        split_axis=0,
        concat_axis=0,
        axis_index_groups=same_core,
        tiled=True,
    )
    return (queued, attended)


def solution(mesh):
    in_specs = (P("band", "tok", None), P("tok", None), P("band"), P(), P(), P(), P(), P())
    out_specs = (P("band", "tok", None), P("band", "tok", None))
    return jax.shard_map(shards, mesh=mesh, in_specs=in_specs, out_specs=out_specs, check_vma=False)
```

```python
import functools
import math

import jax
import jax.numpy as jnp
from jax import lax
from jax.experimental import pallas as pl
from jax.experimental.pallas import tpu as pltpu
from jax.sharding import PartitionSpec as P

HEADS = 8
HD = 72
LANE = 128
WIDTH = HEADS * HD
SHIFT = WIDTH % LANE
OWNERS = (15, 1, 14, 0, 4, 8, 9, 2, 5, 7, 12, 10, 3, 13, 11, 6)
SCALE_LOG2 = math.log2(math.e) / math.sqrt(HD)


def from_behind(block, axis, distance):
    devices = range(lax.axis_size(axis))
    route = [(i - distance, i) for i in devices if i - distance in devices]
    return lax.ppermute(block, axis, route)


def modulation(levels, timesteps, mod_table):
    level_count = timesteps.shape[0]
    one_hot = (levels[:, None] == jnp.arange(level_count, dtype=jnp.int32)[None, :]).astype(
        jnp.int32
    )
    noise_time = jnp.sum(one_hot * timesteps[None, :], axis=1).astype(jnp.float32)
    feature_count = mod_table.shape[1]
    frequency = jnp.exp(
        -math.log(10000.0) * jnp.arange(feature_count, dtype=jnp.float32) / feature_count
    )
    phases = noise_time[:, None] * frequency[None, :]
    offset = mod_table[0][None, :] + jnp.cos(phases)
    stretch = mod_table[1][None, :] + jnp.sin(phases)
    return (offset, stretch)


def project_kernel(
    tokens_hbm, stretch_ref, offset_ref, weight_ref, normed_ref, pair_ref, tokens_ref, arrived
):
    rows = tokens_ref.shape[0]
    step = 128
    copies = [
        pltpu.make_async_copy(
            tokens_hbm.at[pl.ds(i * step, step)], tokens_ref.at[pl.ds(i * step, step)], arrived.at[i]
        )
        for i in range(rows // step)
    ]
    for copy in copies:
        copy.start()
    parts = []
    for i in range(rows // step):
        copies[i].wait()
        values = tokens_ref[pl.ds(i * step, step), :].astype(jnp.float32)
        average = jnp.mean(values, axis=-1, keepdims=True)
        centred = values - average
        spread = jnp.mean(centred * centred, axis=-1, keepdims=True)
        normed = centred * lax.rsqrt(spread + 1e-06)
        normed = (normed * (1.0 + stretch_ref[...]) + offset_ref[...]).astype(jnp.bfloat16)
        normed_ref[pl.ds(i * step, step), :] = normed
        parts.append(normed)
    pair_ref[...] = jnp.dot(
        jnp.concatenate(parts, axis=0), weight_ref[...], preferred_element_type=jnp.float32
    ).astype(jnp.bfloat16)


def normalize_and_project(tokens, stretch, offset, weight):
    vmem = pl.BlockSpec(memory_space=pltpu.VMEM)
    rows, width = tokens.shape[0], weight.shape[1]
    return pl.pallas_call(
        project_kernel,
        out_shape=(
            jax.ShapeDtypeStruct(tokens.shape, jnp.bfloat16),
            jax.ShapeDtypeStruct((rows, width), jnp.bfloat16),
        ),
        in_specs=[pl.BlockSpec(memory_space=pl.ANY)] + [vmem] * 3,
        out_specs=(vmem, vmem),
        scratch_shapes=[
            pltpu.VMEM(tokens.shape, jnp.bfloat16),
            pltpu.SemaphoreType.DMA((rows // 128,)),
        ],
        compiler_params=pltpu.CompilerParams(vmem_limit_bytes=24 * 2**20),
        name="project",
    )(tokens, stretch, offset, weight)


def attention_kernel(query_ref, own_ref, other_ref, out_ref):
    dims = (((1,), (1,)), ((), ()))
    window = 2 * LANE
    rows = query_ref.shape[0]
    lane = lax.broadcasted_iota(jnp.int32, (rows, window), 1)
    pairs = (own_ref, other_ref)
    for head in range(HEADS):
        start = min((SHIFT + head * HD) // LANE * LANE, SHIFT + WIDTH - window)
        first = SHIFT + head * HD - start
        inside = (lane >= first) & (lane < first + HD)
        query = jnp.where(inside, query_ref[:, pl.ds(start, window)], 0)
        scores = [
            lax.dot_general(
                query,
                pair[:, pl.ds(WIDTH - SHIFT + start, window)],
                dims,
                preferred_element_type=jnp.float32,
            )
            for pair in pairs
        ]
        peak = jnp.maximum(*(jnp.max(score, axis=1, keepdims=True) for score in scores))
        start = head * HD // LANE * LANE
        first = head * HD - start
        inside = (lane >= first) & (lane < first + HD)
        total = 0.0
        for score, pair in zip(scores, pairs):
            weight = jnp.exp2((score - peak) * SCALE_LOG2).astype(jnp.bfloat16)
            value = jnp.where(inside, pair[:, pl.ds(start, window)], 1)
            total += jnp.dot(weight, value, preferred_element_type=jnp.float32)
        at = first + HD if first + HD < window else 0
        result = total / total[:, at : at + 1]
        if head == 0:
            done = result
        else:
            if start != done_start:
                out_ref[:, pl.ds(done_start, LANE)] = done[:, :LANE].astype(jnp.bfloat16)
                done = jnp.concatenate([done[:, LANE:], result[:, LANE:]], axis=1)
            done = jnp.where(lane < first, done, result)
        done_start = start
    tail = WIDTH - done_start
    out_ref[:, pl.ds(done_start, tail)] = done[:, :tail].astype(jnp.bfloat16)


def attend(query, own, other):
    vmem = pl.BlockSpec(memory_space=pltpu.VMEM)
    rows = query.shape[0]
    return pl.pallas_call(
        attention_kernel,
        out_shape=jax.ShapeDtypeStruct((rows, WIDTH), jnp.bfloat16),
        in_specs=[vmem] * 3,
        out_specs=vmem,
        compiler_params=pltpu.CompilerParams(vmem_limit_bytes=32 * 2**20),
        name="attention",
    )(query, own, other)


def shards(latents, new_frame, levels, timesteps, mod_table, w_query, w_key, w_value):
    frames, tokens_dev, model_width = latents.shape
    groups = lax.axis_size("tok")
    cores = groups // frames
    same_core = [[cores * chip + core for chip in OWNERS] for core in range(cores)]
    incoming = from_behind(latents[-1:], "band", 1)
    head_frame = jnp.where(lax.axis_index("band") == 0, new_frame[None], incoming)
    moved = lax.optimization_barrier(jnp.concatenate([new_frame[None], latents[:-1]], axis=0))
    queued = lax.dynamic_update_slice_in_dim(moved, head_frame, 0, axis=0)
    mine = lax.all_to_all(
        queued, "tok", split_axis=0, concat_axis=0, axis_index_groups=same_core, tiled=True
    )
    mine = mine.reshape(frames * tokens_dev, model_width)
    chip = lax.axis_index("tok") // cores
    level = jnp.sum(jnp.where(jnp.array(OWNERS) == chip, levels, 0), keepdims=True)
    offset, stretch = modulation(level, timesteps, mod_table)
    w_pair = jnp.concatenate([w_value, w_key], axis=1)
    normed, own = normalize_and_project(mine, stretch, offset, w_pair)
    other = lax.ppermute(own, "tok", [(i, i ^ 1) for i in range(groups)])
    w_shifted = jnp.pad(w_query, ((0, 0), (SHIFT, 0)))
    query = jnp.dot(normed, w_shifted, preferred_element_type=jnp.float32).astype(jnp.bfloat16)
    result = attend(query, own, other)
    attended = lax.all_to_all(
        result.reshape(frames, tokens_dev, WIDTH),
        "tok",
        split_axis=0,
        concat_axis=0,
        axis_index_groups=same_core,
        tiled=True,
    )
    return (queued, attended)


def solution(mesh):
    in_specs = (P("band", "tok", None), P("tok", None), P("band"), P(), P(), P(), P(), P())
    out_specs = (P("band", "tok", None), P("band", "tok", None))
    return jax.shard_map(shards, mesh=mesh, in_specs=in_specs, out_specs=out_specs, check_vma=False)
```

```python
import functools
import math

import jax
import jax.numpy as jnp
from jax import lax
from jax.experimental import pallas as pl
from jax.experimental.pallas import tpu as pltpu
from jax.sharding import PartitionSpec as P

HEADS = 8
HD = 72
LANE = 128
WIDTH = HEADS * HD
SHIFT = WIDTH % LANE
OWNERS = (10, 11, 8, 13, 14, 0, 9, 7, 6, 15, 1, 3, 2, 12, 4, 5)
SCALE_LOG2 = math.log2(math.e) / math.sqrt(HD)


def from_behind(block, axis, distance):
    devices = range(lax.axis_size(axis))
    route = [(i - distance, i) for i in devices if i - distance in devices]
    return lax.ppermute(block, axis, route)


def modulation(levels, timesteps, mod_table):
    level_count = timesteps.shape[0]
    one_hot = (levels[:, None] == jnp.arange(level_count, dtype=jnp.int32)[None, :]).astype(
        jnp.int32
    )
    noise_time = jnp.sum(one_hot * timesteps[None, :], axis=1).astype(jnp.float32)
    feature_count = mod_table.shape[1]
    frequency = jnp.exp(
        -math.log(10000.0) * jnp.arange(feature_count, dtype=jnp.float32) / feature_count
    )
    phases = noise_time[:, None] * frequency[None, :]
    offset = mod_table[0][None, :] + jnp.cos(phases)
    stretch = mod_table[1][None, :] + jnp.sin(phases)
    return (offset, stretch)


def project_kernel(
    tokens_hbm, stretch_ref, offset_ref, weight_ref, normed_ref, pair_ref, tokens_ref, arrived
):
    rows = tokens_ref.shape[0]
    step = 128
    copies = [
        pltpu.make_async_copy(
            tokens_hbm.at[pl.ds(i * step, step)], tokens_ref.at[pl.ds(i * step, step)], arrived.at[i]
        )
        for i in range(rows // step)
    ]
    for copy in copies:
        copy.start()
    parts = []
    for i in range(rows // step):
        copies[i].wait()
        values = tokens_ref[pl.ds(i * step, step), :].astype(jnp.float32)
        average = jnp.mean(values, axis=-1, keepdims=True)
        centred = values - average
        spread = jnp.mean(centred * centred, axis=-1, keepdims=True)
        normed = centred * lax.rsqrt(spread + 1e-06)
        normed = (normed * (1.0 + stretch_ref[...]) + offset_ref[...]).astype(jnp.bfloat16)
        normed_ref[pl.ds(i * step, step), :] = normed
        parts.append(normed)
    pair_ref[...] = jnp.dot(
        jnp.concatenate(parts, axis=0), weight_ref[...], preferred_element_type=jnp.float32
    ).astype(jnp.bfloat16)


def normalize_and_project(tokens, stretch, offset, weight):
    vmem = pl.BlockSpec(memory_space=pltpu.VMEM)
    rows, width = tokens.shape[0], weight.shape[1]
    return pl.pallas_call(
        project_kernel,
        out_shape=(
            jax.ShapeDtypeStruct(tokens.shape, jnp.bfloat16),
            jax.ShapeDtypeStruct((rows, width), jnp.bfloat16),
        ),
        in_specs=[pl.BlockSpec(memory_space=pl.ANY)] + [vmem] * 3,
        out_specs=(vmem, vmem),
        scratch_shapes=[
            pltpu.VMEM(tokens.shape, jnp.bfloat16),
            pltpu.SemaphoreType.DMA((rows // 128,)),
        ],
        compiler_params=pltpu.CompilerParams(vmem_limit_bytes=24 * 2**20),
        name="project",
    )(tokens, stretch, offset, weight)


def attention_kernel(query_ref, own_ref, other_ref, out_ref):
    dims = (((1,), (1,)), ((), ()))
    window = 2 * LANE
    rows = query_ref.shape[0]
    lane = lax.broadcasted_iota(jnp.int32, (rows, window), 1)
    pairs = (own_ref, other_ref)
    for head in range(HEADS):
        start = min((SHIFT + head * HD) // LANE * LANE, SHIFT + WIDTH - window)
        first = SHIFT + head * HD - start
        inside = (lane >= first) & (lane < first + HD)
        query = jnp.where(inside, query_ref[:, pl.ds(start, window)], 0)
        scores = [
            lax.dot_general(
                query,
                pair[:, pl.ds(WIDTH - SHIFT + start, window)],
                dims,
                preferred_element_type=jnp.float32,
            )
            for pair in pairs
        ]
        peak = jnp.maximum(*(jnp.max(score, axis=1, keepdims=True) for score in scores))
        start = head * HD // LANE * LANE
        first = head * HD - start
        inside = (lane >= first) & (lane < first + HD)
        total = 0.0
        for score, pair in zip(scores, pairs):
            weight = jnp.exp2((score - peak) * SCALE_LOG2).astype(jnp.bfloat16)
            value = jnp.where(inside, pair[:, pl.ds(start, window)], 1)
            total += jnp.dot(weight, value, preferred_element_type=jnp.float32)
        at = first + HD if first + HD < window else 0
        result = total / total[:, at : at + 1]
        if head == 0:
            done = result
        else:
            if start != done_start:
                out_ref[:, pl.ds(done_start, LANE)] = done[:, :LANE].astype(jnp.bfloat16)
                done = jnp.concatenate([done[:, LANE:], result[:, LANE:]], axis=1)
            done = jnp.where(lane < first, done, result)
        done_start = start
    tail = WIDTH - done_start
    out_ref[:, pl.ds(done_start, tail)] = done[:, :tail].astype(jnp.bfloat16)


def attend(query, own, other):
    vmem = pl.BlockSpec(memory_space=pltpu.VMEM)
    rows = query.shape[0]
    return pl.pallas_call(
        attention_kernel,
        out_shape=jax.ShapeDtypeStruct((rows, WIDTH), jnp.bfloat16),
        in_specs=[vmem] * 3,
        out_specs=vmem,
        compiler_params=pltpu.CompilerParams(vmem_limit_bytes=32 * 2**20),
        name="attention",
    )(query, own, other)


def shards(latents, new_frame, levels, timesteps, mod_table, w_query, w_key, w_value):
    frames, tokens_dev, model_width = latents.shape
    groups = lax.axis_size("tok")
    cores = groups // frames
    same_core = [[cores * chip + core for chip in OWNERS] for core in range(cores)]
    incoming = from_behind(latents[-1:], "band", 1)
    head_frame = jnp.where(lax.axis_index("band") == 0, new_frame[None], incoming)
    moved = lax.optimization_barrier(jnp.concatenate([new_frame[None], latents[:-1]], axis=0))
    queued = lax.dynamic_update_slice_in_dim(moved, head_frame, 0, axis=0)
    mine = lax.all_to_all(
        queued, "tok", split_axis=0, concat_axis=0, axis_index_groups=same_core, tiled=True
    )
    mine = mine.reshape(frames * tokens_dev, model_width)
    chip = lax.axis_index("tok") // cores
    level = jnp.sum(jnp.where(jnp.array(OWNERS) == chip, levels, 0), keepdims=True)
    offset, stretch = modulation(level, timesteps, mod_table)
    w_pair = jnp.concatenate([w_value, w_key], axis=1)
    normed, own = normalize_and_project(mine, stretch, offset, w_pair)
    other = lax.ppermute(own, "tok", [(i, i ^ 1) for i in range(groups)])
    w_shifted = jnp.pad(w_query, ((0, 0), (SHIFT, 0)))
    query = jnp.dot(normed, w_shifted, preferred_element_type=jnp.float32).astype(jnp.bfloat16)
    result = attend(query, own, other)
    attended = lax.all_to_all(
        result.reshape(frames, tokens_dev, WIDTH),
        "tok",
        split_axis=0,
        concat_axis=0,
        axis_index_groups=same_core,
        tiled=True,
    )
    return (queued, attended)


def solution(mesh):
    in_specs = (P("band", "tok", None), P("tok", None), P("band"), P(), P(), P(), P(), P())
    out_specs = (P("band", "tok", None), P("band", "tok", None))
    return jax.shard_map(shards, mesh=mesh, in_specs=in_specs, out_specs=out_specs, check_vma=False)
```

```python
import functools
import math

import jax
import jax.numpy as jnp
from jax import lax
from jax.experimental import pallas as pl
from jax.experimental.pallas import tpu as pltpu
from jax.sharding import PartitionSpec as P

HEADS = 8
HD = 72
LANE = 128
RUN = 16
WIDTH = HEADS * HD
SHIFT = WIDTH % LANE
OWNERS = (10, 11, 8, 13, 14, 0, 9, 7, 6, 15, 1, 3, 2, 12, 4, 5)
SCALE_LOG2 = math.log2(math.e) / math.sqrt(HD)


def from_behind(block, axis, distance):
    devices = range(lax.axis_size(axis))
    route = [(i - distance, i) for i in devices if i - distance in devices]
    return lax.ppermute(block, axis, route)


def modulation(levels, timesteps, mod_table):
    level_count = timesteps.shape[0]
    one_hot = (levels[:, None] == jnp.arange(level_count, dtype=jnp.int32)[None, :]).astype(
        jnp.int32
    )
    noise_time = jnp.sum(one_hot * timesteps[None, :], axis=1).astype(jnp.float32)
    feature_count = mod_table.shape[1]
    frequency = jnp.exp(
        -math.log(10000.0) * jnp.arange(feature_count, dtype=jnp.float32) / feature_count
    )
    phases = noise_time[:, None] * frequency[None, :]
    offset = mod_table[0][None, :] + jnp.cos(phases)
    stretch = mod_table[1][None, :] + jnp.sin(phases)
    return (offset, stretch)


def project_kernel(
    tokens_hbm, stretch_ref, offset_ref, weight_ref, normed_ref, pair_ref, tokens_ref, arrived
):
    rows = tokens_ref.shape[0]
    step = 128
    copies = [
        pltpu.make_async_copy(
            tokens_hbm.at[pl.ds(i * step, step)], tokens_ref.at[pl.ds(i * step, step)], arrived.at[i]
        )
        for i in range(rows // step)
    ]
    for copy in copies:
        copy.start()
    parts = []
    for i in range(rows // step):
        copies[i].wait()
        values = tokens_ref[pl.ds(i * step, step), :].astype(jnp.float32)
        average = jnp.mean(values, axis=-1, keepdims=True)
        centred = values - average
        spread = jnp.mean(centred * centred, axis=-1, keepdims=True)
        normed = centred * lax.rsqrt(spread + 1e-06)
        normed = (normed * (1.0 + stretch_ref[...]) + offset_ref[...]).astype(jnp.bfloat16)
        normed_ref[pl.ds(i * step, step), :] = normed
        parts.append(normed)
    pair_ref[...] = jnp.dot(
        jnp.concatenate(parts, axis=0), weight_ref[...], preferred_element_type=jnp.float32
    ).astype(jnp.bfloat16)


def normalize_and_project(tokens, stretch, offset, weight):
    vmem = pl.BlockSpec(memory_space=pltpu.VMEM)
    rows, width = tokens.shape[0], weight.shape[1]
    return pl.pallas_call(
        project_kernel,
        out_shape=(
            jax.ShapeDtypeStruct(tokens.shape, jnp.bfloat16),
            jax.ShapeDtypeStruct((rows, width), jnp.bfloat16),
        ),
        in_specs=[pl.BlockSpec(memory_space=pl.ANY)] + [vmem] * 3,
        out_specs=(vmem, vmem),
        scratch_shapes=[
            pltpu.VMEM(tokens.shape, jnp.bfloat16),
            pltpu.SemaphoreType.DMA((rows // 128,)),
        ],
        compiler_params=pltpu.CompilerParams(vmem_limit_bytes=24 * 2**20),
        name="project",
    )(tokens, stretch, offset, weight)


def attention_kernel(query_ref, own_ref, other_ref, out_ref, result_ref):
    dims = (((1,), (1,)), ((), ()))
    window = 2 * LANE
    rows = query_ref.shape[0]
    lane = lax.broadcasted_iota(jnp.int32, (rows, window), 1)
    pairs = (own_ref, other_ref)
    for head in range(HEADS):
        start = min((SHIFT + head * HD) // LANE * LANE, SHIFT + WIDTH - window)
        first = SHIFT + head * HD - start
        inside = (lane >= first) & (lane < first + HD)
        query = jnp.where(inside, query_ref[:, pl.ds(start, window)], 0)
        scores = [
            lax.dot_general(
                query,
                pair[:, pl.ds(WIDTH - SHIFT + start, window)],
                dims,
                preferred_element_type=jnp.float32,
            )
            for pair in pairs
        ]
        peak = jnp.maximum(*(jnp.max(score, axis=1, keepdims=True) for score in scores))
        start = head * HD // LANE * LANE
        first = head * HD - start
        inside = (lane >= first) & (lane < first + HD)
        total = 0.0
        for score, pair in zip(scores, pairs):
            weight = jnp.exp2((score - peak) * SCALE_LOG2).astype(jnp.bfloat16)
            value = jnp.where(inside, pair[:, pl.ds(start, window)], 1)
            total += jnp.dot(weight, value, preferred_element_type=jnp.float32)
        at = first + HD if first + HD < window else 0
        result = total / total[:, at : at + 1]
        if head == 0:
            done = result
        else:
            if start != done_start:
                result_ref[:, pl.ds(done_start, LANE)] = done[:, :LANE].astype(jnp.bfloat16)
                done = jnp.concatenate([done[:, LANE:], result[:, LANE:]], axis=1)
            done = jnp.where(lane < first, done, result)
        done_start = start
    result_ref[:, pl.ds(done_start, window)] = done.astype(jnp.bfloat16)
    runs = result_ref[...].reshape(-1, 2, RUN, result_ref.shape[1])[:, :, :, :WIDTH]
    out_ref[...] = jnp.concatenate([runs[:, 0], runs[:, 1]], axis=-1)


def attend(query, own, other):
    vmem = pl.BlockSpec(memory_space=pltpu.VMEM)
    rows = query.shape[0]
    return pl.pallas_call(
        attention_kernel,
        out_shape=jax.ShapeDtypeStruct((rows // (2 * RUN), RUN, 2 * WIDTH), jnp.bfloat16),
        in_specs=[vmem] * 3,
        out_specs=vmem,
        scratch_shapes=[pltpu.VMEM((rows, pl.cdiv(WIDTH, LANE) * LANE), jnp.bfloat16)],
        compiler_params=pltpu.CompilerParams(vmem_limit_bytes=32 * 2**20),
        name="attention",
    )(query, own, other)


def shards(latents, new_frame, levels, timesteps, mod_table, w_query, w_key, w_value):
    frames, tokens_dev, model_width = latents.shape
    groups = lax.axis_size("tok")
    cores = groups // frames
    same_core = [[cores * chip + core for chip in OWNERS] for core in range(cores)]
    incoming = from_behind(latents[-1:], "band", 1)
    head_frame = jnp.where(lax.axis_index("band") == 0, new_frame[None], incoming)
    moved = lax.optimization_barrier(jnp.concatenate([new_frame[None], latents[:-1]], axis=0))
    queued = lax.dynamic_update_slice_in_dim(moved, head_frame, 0, axis=0)
    mine = lax.all_to_all(
        queued, "tok", split_axis=0, concat_axis=0, axis_index_groups=same_core, tiled=True
    )
    mine = mine.reshape(frames * tokens_dev, model_width)
    chip = lax.axis_index("tok") // cores
    level = jnp.sum(jnp.where(jnp.array(OWNERS) == chip, levels, 0), keepdims=True)
    offset, stretch = modulation(level, timesteps, mod_table)
    w_pair = jnp.concatenate([w_value, w_key], axis=1)
    normed, own = normalize_and_project(mine, stretch, offset, w_pair)
    other = lax.ppermute(own, "tok", [(i, i ^ 1) for i in range(groups)])
    w_shifted = jnp.pad(w_query, ((0, 0), (SHIFT, 0)))
    query = jnp.dot(normed, w_shifted, preferred_element_type=jnp.float32).astype(jnp.bfloat16)
    result = attend(query, own, other)
    back = lax.all_to_all(
        result, "tok", split_axis=0, concat_axis=0, axis_index_groups=same_core, tiled=True
    )
    attended = jnp.concatenate([back[:, :, :WIDTH], back[:, :, WIDTH:]], axis=1)
    return (queued, attended)


def solution(mesh):
    in_specs = (P("band", "tok", None), P("tok", None), P("band"), P(), P(), P(), P(), P())
    out_specs = (P("band", "tok", None), P("band", "tok", None))
    return jax.shard_map(shards, mesh=mesh, in_specs=in_specs, out_specs=out_specs, check_vma=False)
```
